32 devices in a mesh: tm: 8 (over y, x, core), space: 4 (over z).
Axes of the slice: x: 2, y: 2, z: 4, core: 2. Of those that a mesh axis runs over, the one named last changes fastest.
Arguments:
- base: float32 [8, 3, 16, 64, 128], P('tm', None, 'space')
- tangent: float32 [8, 4, 3, 16, 64, 128], P('tm', None, None, 'space')
Outputs:
- correction: float32 [8, 3, 16, 64, 128], P('tm', None, 'space')
- defect: float32 [8, 3, 16, 64, 128], P('tm', None, 'space')
- coefs: float32 [8, 4], P('tm')
All inputs are finite; a program needn't handle non-finite values.
Results may differ from the reference program's by a relative error of at most 0.0003.
Values sent between devices are 32-bit elements; how exact they have to be, the bound alone decides.
A program may use at most 128 MiB of HBM per device.

```python
import jax
import jax.numpy as jnp
from jax import lax

NY = 64
NZ = 128
COLS = 4
STEPS = 3
SEGMENTS = 8
NX = 16


def shared_modes(key):
    keys = jax.random.split(key, 3)
    waves = jax.random.randint(keys[0], (3, 4, 3, 1, 1, 1), 1, 4).astype(jnp.float32)
    phase = jax.random.uniform(keys[1], (4, 3, 1, 1, 1), jnp.float32, -jnp.pi, jnp.pi)
    mixing = jax.random.normal(keys[2], (4, 4), jnp.float32)
    xpos = (jnp.arange(NX).astype(jnp.float32) / NX)[:, None, None]
    ypos = (jnp.arange(NY).astype(jnp.float32) / NY)[None, :, None]
    zpos = (jnp.arange(NZ).astype(jnp.float32) / NZ)[None, None, :]
    modes = jnp.sin(2.0 * jnp.pi * (waves[0] * xpos + waves[1] * ypos + waves[2] * zpos) + phase)
    result = mixing[:, 0, None, None, None, None] * modes[0][None]
    for index_j in range(1, 4):
        result = result + mixing[:, index_j, None, None, None, None] * modes[index_j][None]
    return result


def draw_tangent(key, part):
    modes = shared_modes(key)
    key = jax.random.fold_in(key, 11)
    rate_key, noise_key = jax.random.split(key)
    shape = (SEGMENTS, COLS, 3, NX, NY, NZ)
    rates = jnp.exp(jax.random.uniform(rate_key, (SEGMENTS,), jnp.float32, jnp.log(0.25), jnp.log(0.5)))
    noise = jax.random.normal(noise_key, shape, jnp.float32)
    return modes[None] + rates[:, None, None, None, None, None] * noise


def draw_base(key, part):
    modes = shared_modes(key)
    key = jax.random.fold_in(key, 12)
    weight_key, noise_key = jax.random.split(key)
    weights = jax.random.uniform(weight_key, (SEGMENTS, 4), jnp.float32, -1.0, 1.0)
    shape = (SEGMENTS, 3, NX, NY, NZ)
    noise = 0.3 * jax.random.normal(noise_key, shape, jnp.float32)
    ypos = jnp.arange(NY).astype(jnp.float32) / NY
    laminar = 0.5 * jnp.sin(2.0 * jnp.pi * 4.0 * ypos)[None, :, None]
    first = (jnp.arange(3) == 0).astype(jnp.float32)[:, None, None, None]
    result = noise + first * laminar
    for index_k in range(4):
        result = result + 0.5 * weights[:, index_k, None, None, None, None] * modes[index_k][None]
    return result


def setup_inputs(seed: int = 0) -> dict:
    streams_of = jax.random.split(jax.random.key(seed), 3)
    base = draw_base(jax.random.fold_in(streams_of[2], 71), 0)
    tangent = draw_tangent(jax.random.fold_in(streams_of[2], 71), 0)
    return {"base": base, "tangent": tangent}


time_step = 0.05
viscosity = 0.4
forcing_amp = 1.0
wave_number = 4.0

def advance(padded):
    centre = padded[:, :, 1:-1]
    east = padded[:, :, 2:]
    west = padded[:, :, :-2]
    north = jnp.roll(centre, -1, 3)
    south = jnp.roll(centre, 1, 3)
    upper = jnp.roll(centre, -1, 4)
    lower = jnp.roll(centre, 1, 4)
    grad_x = 0.5 * (east - west)
    grad_y = 0.5 * (north - south)
    grad_z = 0.5 * (upper - lower)
    laplace = east + west + north + south + upper + lower - 6.0 * centre
    flow = centre[0]
    advect = flow[0] * grad_x + flow[1] * grad_y + flow[2] * grad_z
    change = viscosity * laplace - advect
    tangents = centre[1:]
    stretch = tangents[:, 0:1] * grad_x[0] + tangents[:, 1:2] * grad_y[0] + tangents[:, 2:3] * grad_z[0]
    ylen = centre.shape[3]
    height = jnp.arange(ylen).astype(centre.dtype)
    drive = forcing_amp * jnp.sin(2.0 * jnp.pi * wave_number * height / ylen)[:, None]
    flow_change = change[0].at[0].add(drive)
    flow_new = flow + time_step * flow_change
    tangent_new = tangents + time_step * (change[1:] - stretch)
    return jnp.concatenate((flow_new[None], tangent_new), 0)

def compose(later, earlier):
    matrix = jnp.dot(later[:, :-1], earlier[:, :-1], precision=lax.Precision.HIGHEST)
    offset = jnp.dot(later[:, :-1], earlier[:, -1], precision=lax.Precision.HIGHEST) + later[:, -1]
    return jnp.concatenate((matrix, offset[:, None]), 1)

def combine(block, weights):
    return jnp.tensordot(weights, block, axes=1, precision=lax.Precision.HIGHEST)

def reference(base, tangent):

    def push(pair):
        fields = jnp.concatenate((pair[0][None], pair[1]), 0)
        for repeat in range(STEPS):
            padded = jnp.concatenate((fields[:, :, -1:], fields, fields[:, :, :1]), 2)
            fields = advance(padded)
        return fields
    pushed_all = lax.map(push, (base, tangent))
    end_state = pushed_all[:, 0]
    pushed = pushed_all[:, 1:]
    tangent_next = jnp.roll(tangent, -1, 0)
    base_next = jnp.roll(base, -1, 0)

    def reduce_maps(group):
        basis_next, pushed_one, end_one, start_next = group
        basis_rows = basis_next.reshape(COLS, -1)
        targets = jnp.concatenate((pushed_one.reshape(COLS, -1), (end_one - start_next).reshape(1, -1)), 0)
        numbers = (((1,), (1,)), ((), ()))
        gram_matrix = lax.dot_general(basis_rows, basis_rows, numbers, precision=lax.Precision.HIGHEST)
        cross_terms = lax.dot_general(basis_rows, targets, numbers, precision=lax.Precision.HIGHEST)
        return jnp.linalg.solve(gram_matrix, cross_terms)
    affine = lax.map(reduce_maps, (tangent_next, pushed, end_state, base_next))
    composite = jnp.concatenate((jnp.eye(COLS, dtype=jnp.float32), jnp.zeros((COLS, 1), jnp.float32)), 1)
    for index_k in range(SEGMENTS):
        composite = compose(affine[index_k], composite)
    start_coef = jnp.linalg.solve(jnp.eye(COLS, dtype=jnp.float32) - composite[:, :-1], composite[:, -1])

    def advance_coef(carry, single):
        following = jnp.dot(single[:, :-1], carry, precision=lax.Precision.HIGHEST) + single[:, -1]
        return (following, carry)
    last_coef, coefs = lax.scan(advance_coef, start_coef, affine)
    coefs_next = jnp.roll(coefs, -1, 0)
    correction = lax.map(lambda pair: combine(pair[0], pair[1]), (tangent, coefs))

    def mismatch(group):
        end_one, pushed_one, own_coefs, start_next, basis_next, next_coefs = group
        return end_one + combine(pushed_one, own_coefs) - start_next - combine(basis_next, next_coefs)
    defect = lax.map(mismatch, (end_state, pushed, coefs, base_next, tangent_next, coefs_next))
    return (correction, defect, coefs)
```

```python
import functools

import jax
import jax.numpy as jnp
from jax import lax
from jax.experimental import pallas as pl
from jax.experimental.pallas import tpu as pltpu
from jax.sharding import PartitionSpec as P

MESH = pl.DeviceIdType.MESH
STEPS = 3
COLS = 4
LANES = 128
GRAM = COLS * COLS
ENTRIES = GRAM + COLS * (COLS + 1)
ROWS = 40

time_step = 0.05
viscosity = 0.4
forcing_amp = 1.0
wave_number = 4.0

KEEP = 1.0 - 6.0 * time_step * viscosity
SPREAD = time_step * viscosity
HALF = 0.5 * time_step


def neighbours(ref, lead, plane):
    centre = ref[(*lead, plane)]
    rows, lanes = centre.shape
    east = ref[(*lead, plane + 1)]
    west = ref[(*lead, plane - 1)]
    north = pltpu.roll(centre, rows - 1, 0)
    south = pltpu.roll(centre, 1, 0)
    upper = pltpu.roll(centre, lanes - 1, 1)
    lower = pltpu.roll(centre, 1, 1)
    total = (east + west) + (north + south) + (upper + lower)
    return centre, total, east - west, north - south, upper - lower


def dot_tiles(a, b):
    prod = a * b
    return jnp.sum(prod.reshape(prod.shape[0] // 8, 8, prod.shape[1]), axis=0)


def eliminate(rows, pivoting):
    rows = [list(r) for r in rows]
    n = len(rows)
    for k in range(n):
        if pivoting:
            for r in range(k + 1, n):
                swap = jnp.abs(rows[r][k]) > jnp.abs(rows[k][k])
                for c in range(k, len(rows[k])):
                    high, low = rows[k][c], rows[r][c]
                    rows[k][c] = jnp.where(swap, low, high)
                    rows[r][c] = jnp.where(swap, high, low)
        inverse = 1.0 / rows[k][k]
        for c in range(k + 1, len(rows[k])):
            rows[k][c] = rows[k][c] * inverse
        for r in range(n):
            if r != k:
                factor = rows[r][k]
                for c in range(k + 1, len(rows[k])):
                    rows[r][c] = rows[r][c] - factor * rows[k][c]
    return [r[n:] for r in rows]


def shooting_coefs(entry, n_tm):
    def roll(x, by):
        return pltpu.roll(x, by % LANES, 1)

    gram = [[roll(entry(a * COLS + b), -1) for b in range(COLS)] for a in range(COLS)]
    cross = [[entry(GRAM + k * COLS + j) for k in range(COLS + 1)] for j in range(COLS)]
    maps = eliminate([g + c for g, c in zip(gram, cross)], False)
    maps = [[roll(x, 1) for x in row] for row in maps]
    for level in range(n_tm.bit_length() - 1):
        earlier = [[roll(x, 1 << level) for x in row] for row in maps]
        new = []
        for r in range(COLS):
            row = []
            for c in range(COLS + 1):
                terms = [maps[r][k] * earlier[k][c] for k in range(COLS)]
                value = (terms[0] + terms[1]) + (terms[2] + terms[3])
                row.append(value + maps[r][COLS] if c == COLS else value)
            new.append(row)
        maps = new
    system = [
        [(1.0 if r == c else 0.0) - maps[r][c] for c in range(COLS)] + [maps[r][COLS]]
        for r in range(COLS)
    ]
    return [r[0] for r in eliminate(system, True)]


def kernel(
    n_tm, n_space, base_ref, tangent_ref, corr_ref, defect_ref, coefs_ref,
    flow, grads, tang, work, push, base_next, tang_next, acc, share, table,
    corr, defect,
    local_sem, send_sem, recv_sem, tm_send, tm_recv,
    share_send, share_recv, table_send, table_recv, out_sem,
):
    tm, space = lax.axis_index("tm"), lax.axis_index("space")
    nx = base_ref.shape[2]
    ny, nz = base_ref.shape[3:]
    wide = nx + 2 * STEPS
    up, down = lax.rem(space + 1, n_space), lax.rem(space + n_space - 1, n_space)
    before = lax.rem(tm + n_tm - 1, n_tm)

    barrier = pltpu.get_barrier_semaphore()
    for d in range(1, n_space):
        pl.semaphore_signal(
            barrier, inc=1, device_id={"space": lax.rem(space + d, n_space)}, device_id_type=MESH
        )
    for d in range(1, n_tm):
        pl.semaphore_signal(
            barrier, inc=1, device_id={"tm": lax.rem(tm + d, n_tm)}, device_id_type=MESH
        )
    own = pl.ds(STEPS, nx)
    local = [
        pltpu.make_async_copy(base_ref.at[0], flow.at[0, :, own], local_sem.at[0]),
        pltpu.make_async_copy(tangent_ref.at[0], tang.at[:, :, own], local_sem.at[1]),
    ]
    for copy in local:
        copy.start()
    pl.semaphore_wait(barrier, n_space + n_tm - 2)

    def halo(chunk, side):
        source = pl.ds(nx - STEPS, STEPS) if side == 0 else pl.ds(0, STEPS)
        target = pl.ds(0, STEPS) if side == 0 else pl.ds(nx + STEPS, STEPS)
        if isinstance(chunk, int) and chunk == 0:
            src, dst = base_ref.at[0, :, source], flow.at[0, :, target]
        else:
            src, dst = tangent_ref.at[0, chunk - 1, :, source], tang.at[chunk - 1, :, target]
        return pltpu.make_async_remote_copy(
            src_ref=src, dst_ref=dst,
            send_sem=send_sem.at[chunk, side], recv_sem=recv_sem.at[chunk, side],
            device_id={"space": up if side == 0 else down}, device_id_type=MESH,
        )

    def tm_copy(which):
        src, dst = ((base_ref.at[0], base_next), (tangent_ref.at[0], tang_next))[which]
        return pltpu.make_async_remote_copy(
            src_ref=src, dst_ref=dst, send_sem=tm_send.at[which], recv_sem=tm_recv.at[which],
            device_id={"tm": before}, device_id_type=MESH,
        )

    for chunk in (0, 1):
        for side in (0, 1):
            halo(chunk, side).start()
    for which in (0, 1):
        tm_copy(which).start()

    height = lax.broadcasted_iota(jnp.int32, (ny, nz), 0).astype(jnp.float32)
    drive = (time_step * forcing_amp) * jnp.sin(2.0 * jnp.pi * wave_number * height / ny)

    for copy in local:
        copy.wait()
    acc[...] = jnp.zeros_like(acc)
    pairs = [(a, b) for a in range(COLS) for b in range(a, COLS)]

    def gram_step(i, sums):
        comp, plane = i // nx, i % nx + STEPS
        cols = [tang[k, comp, plane] for k in range(COLS)]
        return tuple(s + dot_tiles(cols[a], cols[b]) for s, (a, b) in zip(sums, pairs))

    zero = jnp.zeros((8, nz), jnp.float32)
    sums = lax.fori_loop(0, 3 * nx, gram_step, (zero,) * len(pairs))
    for s, (a, b) in zip(sums, pairs):
        acc[a * COLS + b] = s
        if a != b:
            acc[b * COLS + a] = s

    for side in (0, 1):
        halo(0, side).wait()
    for side in (0, 1):
        halo(2, side).start()
    for t in range(STEPS):

        def flow_step(plane, carry):
            speed = [HALF * flow[t, d, plane] for d in range(3)]
            for c in range(3):
                centre, total, *diffs = neighbours(flow, (t, c), plane)
                value = KEEP * centre + SPREAD * total
                value = value - (speed[0] * diffs[0] + speed[1] * diffs[1] + speed[2] * diffs[2])
                if c == 0:
                    value = value + drive
                flow[t + 1, c, plane] = value
                for d in range(3):
                    grads[t, 3 * c + d, plane] = HALF * diffs[d]
            return carry

        lax.fori_loop(t + 1, wide - t - 1, flow_step, 0)

    for which in (0, 1):
        tm_copy(which).wait()

    def end_step(i, sums):
        comp, plane = i // nx, i % nx
        gap = flow[STEPS, comp, plane + STEPS] - base_next[comp, plane]
        base_next[comp, plane] = gap
        return tuple(s + dot_tiles(tang_next[j, comp, plane], gap) for j, s in enumerate(sums))

    sums = lax.fori_loop(0, 3 * nx, end_step, (zero,) * COLS)
    for j, s in enumerate(sums):
        acc[GRAM + COLS * COLS + j] = s

    def column(k, carry):
        for side in (0, 1):
            halo(k + 1, side).wait()

        @pl.when(k + 3 < COLS + 1)
        def _():
            for side in (0, 1):
                halo(k + 3, side).start()

        for t in range(STEPS):

            def tangent_step(plane, sums):
                src, lead = (tang, (k,)) if t == 0 else (work, (t - 1,))
                speed = [HALF * flow[t, d, plane] for d in range(3)]
                own_at = [src[(*lead, d, plane)] for d in range(3)]
                for c in range(3):
                    centre, total, *diffs = neighbours(src, (*lead, c), plane)
                    value = KEEP * centre + SPREAD * total
                    value = value - (
                        speed[0] * diffs[0] + speed[1] * diffs[1] + speed[2] * diffs[2]
                    )
                    value = value - (
                        own_at[0] * grads[t, 3 * c, plane]
                        + own_at[1] * grads[t, 3 * c + 1, plane]
                        + own_at[2] * grads[t, 3 * c + 2, plane]
                    )
                    if t < STEPS - 1:
                        work[t, c, plane] = value
                    else:
                        push[k, c, plane - STEPS] = value
                        sums = tuple(
                            s + dot_tiles(tang_next[j, c, plane - STEPS], value)
                            for j, s in enumerate(sums)
                        )
                return sums

            last = t == STEPS - 1
            sums = lax.fori_loop(
                t + 1, wide - t - 1, tangent_step, (zero,) * COLS if last else ()
            )
        for j, s in enumerate(sums):
            acc[GRAM + k * COLS + j] = s
        return carry

    lax.fori_loop(0, COLS, column, 0)

    by_entry = jnp.sum(jnp.sum(acc[...], axis=1), axis=1, keepdims=True)
    row_id = lax.broadcasted_iota(jnp.int32, (ROWS, LANES), 0)
    lane_id = lax.broadcasted_iota(jnp.int32, (ROWS, LANES), 1)
    packed = jnp.sum(jnp.where(row_id == lane_id, by_entry, 0.0), axis=0, keepdims=True)
    share[space] = jnp.broadcast_to(packed, (8, LANES))

    def share_copy(d):
        return pltpu.make_async_remote_copy(
            src_ref=share.at[space], dst_ref=share.at[space],
            send_sem=share_send.at[d], recv_sem=share_recv.at[d],
            device_id={"space": lax.rem(space + d, n_space)}, device_id_type=MESH,
        )

    def table_copy(d):
        return pltpu.make_async_remote_copy(
            src_ref=table.at[tm], dst_ref=table.at[tm],
            send_sem=table_send.at[d], recv_sem=table_recv.at[d],
            device_id={"tm": lax.rem(tm + d, n_tm)}, device_id_type=MESH,
        )

    for d in range(1, n_space):
        share_copy(d).start()
    for d in range(1, n_space):
        share_copy(d).wait()
    table[tm] = functools.reduce(jnp.add, [share[s] for s in range(n_space)])
    for d in range(1, n_tm):
        table_copy(d).start()
    for d in range(1, n_tm):
        table_copy(d).wait()

    sub = lax.broadcasted_iota(jnp.int32, (8, LANES), 0)
    groups = []
    for g in range(max(n_tm // 8, 1)):
        tile = jnp.zeros((8, LANES), jnp.float32)
        for s in range(8):
            tile = jnp.where(sub == s, table[(8 * g + s) % n_tm], tile)
        groups.append(tile)
    square = jnp.concatenate(groups * (LANES // (8 * len(groups))), axis=0)
    flipped = square.T
    coefs = shooting_coefs(lambda e: flipped[e : e + 1], n_tm)

    lane = lax.broadcasted_iota(jnp.int32, (1, LANES), 1)
    mine = lane == tm
    following = lane == lax.rem(tm + 1, n_tm)
    both = jnp.concatenate(
        [jnp.where(mine, x, 0.0) for x in coefs] + [jnp.where(following, x, 0.0) for x in coefs],
        axis=0,
    )
    values = jnp.sum(both, axis=1, keepdims=True)
    own_c = [values[k : k + 1] for k in range(COLS)]
    next_c = [values[COLS + k : COLS + k + 1] for k in range(COLS)]
    places = lax.broadcasted_iota(jnp.int32, (1, COLS), 1)
    out = jnp.zeros((1, COLS), jnp.float32)
    for k in range(COLS):
        out = jnp.where(places == k, own_c[k], out)
    coefs_ref[...] = out

    def out_copy(which, comp):
        src, dst = ((corr, corr_ref), (defect, defect_ref))[which]
        return pltpu.make_async_copy(src.at[comp], dst.at[0, comp], out_sem.at[which, comp])

    own_b = [jnp.broadcast_to(x, (8, LANES)) for x in own_c]
    next_b = [jnp.broadcast_to(x, (8, LANES)) for x in next_c]

    def scaled(coef, array):
        return (array.reshape(ny // 8, 8, nz) * coef[None]).reshape(ny, nz)

    for comp in range(3):

        def finish(plane, carry):
            terms = [scaled(own_b[k], tang[k, comp, plane + STEPS]) for k in range(COLS)]
            corr[comp, plane] = (terms[0] + terms[1]) + (terms[2] + terms[3])
            value = base_next[comp, plane]
            for k in range(COLS):
                value = value + (
                    scaled(own_b[k], push[k, comp, plane])
                    - scaled(next_b[k], tang_next[k, comp, plane])
                )
            defect[comp, plane] = value
            return carry

        lax.fori_loop(0, nx, finish, 0)
        out_copy(0, comp).start()
        out_copy(1, comp).start()
    for comp in range(3):
        out_copy(0, comp).wait()
        out_copy(1, comp).wait()


def body(n_tm, n_space, base, tangent):
    _, comps, nx, ny, nz = base.shape
    wide = nx + 2 * STEPS
    f32 = jnp.float32
    vmem = pltpu.VMEM
    dma = pltpu.SemaphoreType.DMA
    anywhere = pl.BlockSpec(memory_space=pl.ANY)
    return pl.pallas_call(
        functools.partial(kernel, n_tm, n_space),
        out_shape=(
            jax.ShapeDtypeStruct(base.shape, f32),
            jax.ShapeDtypeStruct(base.shape, f32),
            jax.ShapeDtypeStruct((1, COLS), f32),
        ),
        in_specs=[anywhere, anywhere],
        out_specs=(anywhere, anywhere, pl.BlockSpec(memory_space=pltpu.VMEM)),
        scratch_shapes=[
            vmem((STEPS + 1, comps, wide, ny, nz), f32),
            vmem((STEPS, 3 * comps, wide, ny, nz), f32),
            vmem((COLS, comps, wide, ny, nz), f32),
            vmem((STEPS - 1, comps, wide, ny, nz), f32),
            vmem((COLS, comps, nx, ny, nz), f32),
            vmem((comps, nx, ny, nz), f32),
            vmem((COLS, comps, nx, ny, nz), f32),
            vmem((ROWS, 8, nz), f32),
            vmem((n_space, 8, LANES), f32),
            vmem((n_tm, 8, LANES), f32),
            vmem((comps, nx, ny, nz), f32),
            vmem((comps, nx, ny, nz), f32),
            dma((2,)),
            dma((COLS + 1, 2)),
            dma((COLS + 1, 2)),
            dma((2,)),
            dma((2,)),
            dma((n_space,)),
            dma((n_space,)),
            dma((n_tm,)),
            dma((n_tm,)),
            dma((2, comps)),
        ],
        compiler_params=pltpu.CompilerParams(
            collective_id=0, has_side_effects=True, vmem_limit_bytes=44 << 20
        ),
    )(base, tangent)


def solution(mesh):
    return jax.shard_map(
        functools.partial(body, mesh.shape["tm"], mesh.shape["space"]),
        mesh=mesh,
        in_specs=(P("tm", None, "space", None, None), P("tm", None, None, "space", None, None)),
        out_specs=(
            P("tm", None, "space", None, None),
            P("tm", None, "space", None, None),
            P("tm", None),
        ),
        check_vma=False,
    )
```

```python
import functools

import jax
import jax.numpy as jnp
from jax import lax
from jax.experimental import pallas as pl
from jax.experimental.pallas import tpu as pltpu
from jax.sharding import PartitionSpec as P

MESH = pl.DeviceIdType.MESH
STEPS = 3
COLS = 4
LANES = 128
GRAM = COLS * COLS
ENTRIES = GRAM + COLS * (COLS + 1)
ROWS = 40

time_step = 0.05
viscosity = 0.4
forcing_amp = 1.0
wave_number = 4.0

KEEP = 1.0 - 6.0 * time_step * viscosity
SPREAD = time_step * viscosity
HALF = 0.5 * time_step


def neighbours(ref, lead, plane):
    centre = ref[(*lead, plane)]
    rows, lanes = centre.shape
    east = ref[(*lead, plane + 1)]
    west = ref[(*lead, plane - 1)]
    north = pltpu.roll(centre, rows - 1, 0)
    south = pltpu.roll(centre, 1, 0)
    upper = pltpu.roll(centre, lanes - 1, 1)
    lower = pltpu.roll(centre, 1, 1)
    total = (east + west) + (north + south) + (upper + lower)
    return centre, total, east - west, north - south, upper - lower


def dot_tiles(a, b):
    prod = a * b
    return jnp.sum(prod.reshape(prod.shape[0] // 8, 8, prod.shape[1]), axis=0)


def eliminate(rows, pivoting):
    rows = [list(r) for r in rows]
    n = len(rows)
    for k in range(n):
        if pivoting:
            for r in range(k + 1, n):
                swap = jnp.abs(rows[r][k]) > jnp.abs(rows[k][k])
                for c in range(k, len(rows[k])):
                    high, low = rows[k][c], rows[r][c]
                    rows[k][c] = jnp.where(swap, low, high)
                    rows[r][c] = jnp.where(swap, high, low)
        inverse = 1.0 / rows[k][k]
        for c in range(k + 1, len(rows[k])):
            rows[k][c] = rows[k][c] * inverse
        for r in range(n):
            if r != k:
                factor = rows[r][k]
                for c in range(k + 1, len(rows[k])):
                    rows[r][c] = rows[r][c] - factor * rows[k][c]
    return [r[n:] for r in rows]


def shooting_coefs(entry, n_tm):
    def roll(x, by):
        return pltpu.roll(x, by % LANES, 1)

    gram = [[roll(entry(a * COLS + b), -1) for b in range(COLS)] for a in range(COLS)]
    cross = [[entry(GRAM + k * COLS + j) for k in range(COLS + 1)] for j in range(COLS)]
    maps = eliminate([g + c for g, c in zip(gram, cross)], False)
    maps = [[roll(x, 1) for x in row] for row in maps]
    for level in range(n_tm.bit_length() - 1):
        earlier = [[roll(x, 1 << level) for x in row] for row in maps]
        new = []
        for r in range(COLS):
            row = []
            for c in range(COLS + 1):
                terms = [maps[r][k] * earlier[k][c] for k in range(COLS)]
                value = (terms[0] + terms[1]) + (terms[2] + terms[3])
                row.append(value + maps[r][COLS] if c == COLS else value)
            new.append(row)
        maps = new
    system = [
        [(1.0 if r == c else 0.0) - maps[r][c] for c in range(COLS)] + [maps[r][COLS]]
        for r in range(COLS)
    ]
    return [r[0] for r in eliminate(system, True)]


def kernel(
    n_tm, n_space, base_ref, tangent_ref, corr_ref, defect_ref, coefs_ref,
    flow, grads, tang, work, push, base_next, tang_next, acc, table,
    corr, defect,
    local_sem, send_sem, recv_sem, tm_send, tm_recv,
    table_send, table_recv, out_sem,
):
    tm, space = lax.axis_index("tm"), lax.axis_index("space")
    nx = base_ref.shape[2]
    ny, nz = base_ref.shape[3:]
    wide = nx + 2 * STEPS
    up, down = lax.rem(space + 1, n_space), lax.rem(space + n_space - 1, n_space)
    before = lax.rem(tm + n_tm - 1, n_tm)

    barrier = pltpu.get_barrier_semaphore()
    order = sorted(range(n_space), key=lambda d: (d in (0,), min(d, n_space - d)))
    others = [(d, e) for d in order for e in range(n_tm) if (d, e) != (0, 0)]

    def other(offset):
        d, e = offset
        return {"tm": lax.rem(tm + e, n_tm), "space": lax.rem(space + d, n_space)}

    for offset in others:
        pl.semaphore_signal(barrier, inc=1, device_id=other(offset), device_id_type=MESH)
    own = pl.ds(STEPS, nx)
    local = [
        pltpu.make_async_copy(base_ref.at[0], flow.at[0, :, own], local_sem.at[0]),
        pltpu.make_async_copy(tangent_ref.at[0], tang.at[:, :, own], local_sem.at[1]),
    ]
    for copy in local:
        copy.start()
    pl.semaphore_wait(barrier, len(others))

    def halo(chunk, part, side):
        near = STEPS - 1
        source = (
            (pl.ds(nx - near, near), pl.ds(0, near)),
            (pl.ds(nx - STEPS, 1), pl.ds(near, 1)),
        )[part][side]
        target = (
            (pl.ds(1, near), pl.ds(nx + STEPS, near)),
            (pl.ds(0, 1), pl.ds(wide - 1, 1)),
        )[part][side]
        if isinstance(chunk, int) and chunk == 0:
            src, dst = base_ref.at[0, :, source], flow.at[0, :, target]
        else:
            src, dst = tangent_ref.at[0, chunk - 1, :, source], tang.at[chunk - 1, :, target]
        return pltpu.make_async_remote_copy(
            src_ref=src, dst_ref=dst,
            send_sem=send_sem.at[chunk, part, side], recv_sem=recv_sem.at[chunk, part, side],
            device_id={"space": up if side == 0 else down}, device_id_type=MESH,
        )

    def tm_copy(which):
        src, dst = ((base_ref.at[0], base_next), (tangent_ref.at[0], tang_next))[which]
        return pltpu.make_async_remote_copy(
            src_ref=src, dst_ref=dst, send_sem=tm_send.at[which], recv_sem=tm_recv.at[which],
            device_id={"tm": before}, device_id_type=MESH,
        )

    for chunk in range(COLS + 1):
        for part in (0, 1):
            for side in (0, 1):
                halo(chunk, part, side).start()
    for which in (0, 1):
        tm_copy(which).start()

    height = lax.broadcasted_iota(jnp.int32, (ny, nz), 0).astype(jnp.float32)
    drive = (time_step * forcing_amp) * jnp.sin(2.0 * jnp.pi * wave_number * height / ny)

    for copy in local:
        copy.wait()
    acc[...] = jnp.zeros_like(acc)
    pairs = [(a, b) for a in range(COLS) for b in range(a, COLS)]

    def gram_step(i, sums):
        comp, plane = i // nx, i % nx + STEPS
        cols = [tang[k, comp, plane] for k in range(COLS)]
        return tuple(s + dot_tiles(cols[a], cols[b]) for s, (a, b) in zip(sums, pairs))

    zero = jnp.zeros((8, nz), jnp.float32)
    sums = lax.fori_loop(0, 3 * nx, gram_step, (zero,) * len(pairs))
    for s, (a, b) in zip(sums, pairs):
        acc[a * COLS + b] = s
        if a != b:
            acc[b * COLS + a] = s

    for part in (0, 1):
        for side in (0, 1):
            halo(0, part, side).wait()
    for t in range(STEPS):

        def flow_step(plane, carry):
            speed = [HALF * flow[t, d, plane] for d in range(3)]
            for c in range(3):
                centre, total, *diffs = neighbours(flow, (t, c), plane)
                value = KEEP * centre + SPREAD * total
                value = value - (speed[0] * diffs[0] + speed[1] * diffs[1] + speed[2] * diffs[2])
                if c == 0:
                    value = value + drive
                flow[t + 1, c, plane] = value
                for d in range(3):
                    grads[t, 3 * c + d, plane] = HALF * diffs[d]
            return carry

        lax.fori_loop(t + 1, wide - t - 1, flow_step, 0)

    for which in (0, 1):
        tm_copy(which).wait()

    def end_step(i, sums):
        comp, plane = i // nx, i % nx
        gap = flow[STEPS, comp, plane + STEPS] - base_next[comp, plane]
        base_next[comp, plane] = gap
        return tuple(s + dot_tiles(tang_next[j, comp, plane], gap) for j, s in enumerate(sums))

    sums = lax.fori_loop(0, 3 * nx, end_step, (zero,) * COLS)
    for j, s in enumerate(sums):
        acc[GRAM + COLS * COLS + j] = s

    def column(k, carry):
        def tangent_step(t, plane, sums):
            src, lead = (tang, (k,)) if t == 0 else (work, (t - 1,))
            speed = [HALF * flow[t, d, plane] for d in range(3)]
            own_at = [src[(*lead, d, plane)] for d in range(3)]
            for c in range(3):
                centre, total, *diffs = neighbours(src, (*lead, c), plane)
                value = KEEP * centre + SPREAD * total
                value = value - (
                    speed[0] * diffs[0] + speed[1] * diffs[1] + speed[2] * diffs[2]
                )
                value = value - (
                    own_at[0] * grads[t, 3 * c, plane]
                    + own_at[1] * grads[t, 3 * c + 1, plane]
                    + own_at[2] * grads[t, 3 * c + 2, plane]
                )
                if t < STEPS - 1:
                    work[t, c, plane] = value
                else:
                    push[k, c, plane - STEPS] = value
                    sums = tuple(
                        s + dot_tiles(tang_next[j, c, plane - STEPS], value)
                        for j, s in enumerate(sums)
                    )
            return sums

        sums = (zero,) * COLS
        for part in (0, 1):
            for side in (0, 1):
                halo(k + 1, part, side).wait()
            for t in range(STEPS):
                carried = sums if t == STEPS - 1 else ()
                first, last = t + 1, wide - t - 2
                if part == 0:
                    done = lax.fori_loop(
                        first + 1, last, functools.partial(tangent_step, t), carried
                    )
                else:
                    done = lax.fori_loop(
                        0, 2,
                        lambda i, x, t=t, first=first, last=last: tangent_step(
                            t, first + i * (last - first), x
                        ),
                        carried,
                    )
                if t == STEPS - 1:
                    sums = done
        for j, s in enumerate(sums):
            acc[GRAM + k * COLS + j] = s
        return carry

    lax.fori_loop(0, COLS, column, 0)

    by_entry = jnp.sum(jnp.sum(acc[...], axis=1), axis=1, keepdims=True)
    row_id = lax.broadcasted_iota(jnp.int32, (ROWS, LANES), 0)
    lane_id = lax.broadcasted_iota(jnp.int32, (ROWS, LANES), 1)
    packed = jnp.sum(jnp.where(row_id == lane_id, by_entry, 0.0), axis=0, keepdims=True)
    table[space, pl.ds(tm, 1)] = packed

    def table_copy(index):
        row = table.at[space, pl.ds(tm, 1)]
        return pltpu.make_async_remote_copy(
            src_ref=row, dst_ref=row, send_sem=table_send.at[index], recv_sem=table_recv.at[index],
            device_id=other(others[index]), device_id_type=MESH,
        )

    for index in range(len(others)):
        table_copy(index).start()
    for index in range(len(others)):
        table_copy(index).wait()
    summed = functools.reduce(jnp.add, [table[d] for d in range(n_space)])
    square = jnp.concatenate([summed] * (LANES // n_tm), axis=0)
    flipped = square.T
    coefs = shooting_coefs(lambda e: flipped[e : e + 1], n_tm)

    lane = lax.broadcasted_iota(jnp.int32, (1, LANES), 1)
    mine = lane == tm
    following = lane == lax.rem(tm + 1, n_tm)
    both = jnp.concatenate(
        [jnp.where(mine, x, 0.0) for x in coefs] + [jnp.where(following, x, 0.0) for x in coefs],
        axis=0,
    )
    values = jnp.sum(both, axis=1, keepdims=True)
    own_c = [values[k : k + 1] for k in range(COLS)]
    next_c = [values[COLS + k : COLS + k + 1] for k in range(COLS)]
    places = lax.broadcasted_iota(jnp.int32, (1, COLS), 1)
    out = jnp.zeros((1, COLS), jnp.float32)
    for k in range(COLS):
        out = jnp.where(places == k, own_c[k], out)
    coefs_ref[...] = out

    def out_copy(which, comp):
        src, dst = ((corr, corr_ref), (defect, defect_ref))[which]
        return pltpu.make_async_copy(src.at[comp], dst.at[0, comp], out_sem.at[which, comp])

    own_b = [jnp.broadcast_to(x, (8, LANES)) for x in own_c]
    next_b = [jnp.broadcast_to(x, (8, LANES)) for x in next_c]

    def scaled(coef, array):
        return (array.reshape(ny // 8, 8, nz) * coef[None]).reshape(ny, nz)

    for comp in range(3):

        def finish(plane, carry):
            terms = [scaled(own_b[k], tang[k, comp, plane + STEPS]) for k in range(COLS)]
            corr[comp, plane] = (terms[0] + terms[1]) + (terms[2] + terms[3])
            value = base_next[comp, plane]
            for k in range(COLS):
                value = value + (
                    scaled(own_b[k], push[k, comp, plane])
                    - scaled(next_b[k], tang_next[k, comp, plane])
                )
            defect[comp, plane] = value
            return carry

        lax.fori_loop(0, nx, finish, 0)
        out_copy(0, comp).start()
        out_copy(1, comp).start()
    for comp in range(3):
        out_copy(0, comp).wait()
        out_copy(1, comp).wait()


def body(n_tm, n_space, base, tangent):
    _, comps, nx, ny, nz = base.shape
    wide = nx + 2 * STEPS
    f32 = jnp.float32
    vmem = pltpu.VMEM
    dma = pltpu.SemaphoreType.DMA
    anywhere = pl.BlockSpec(memory_space=pl.ANY)
    return pl.pallas_call(
        functools.partial(kernel, n_tm, n_space),
        out_shape=(
            jax.ShapeDtypeStruct(base.shape, f32),
            jax.ShapeDtypeStruct(base.shape, f32),
            jax.ShapeDtypeStruct((1, COLS), f32),
        ),
        in_specs=[anywhere, anywhere],
        out_specs=(anywhere, anywhere, pl.BlockSpec(memory_space=pltpu.VMEM)),
        scratch_shapes=[
            vmem((STEPS + 1, comps, wide, ny, nz), f32),
            vmem((STEPS, 3 * comps, wide, ny, nz), f32),
            vmem((COLS, comps, wide, ny, nz), f32),
            vmem((STEPS - 1, comps, wide, ny, nz), f32),
            vmem((COLS, comps, nx, ny, nz), f32),
            vmem((comps, nx, ny, nz), f32),
            vmem((COLS, comps, nx, ny, nz), f32),
            vmem((ROWS, 8, nz), f32),
            vmem((n_space, n_tm, LANES), f32),
            vmem((comps, nx, ny, nz), f32),
            vmem((comps, nx, ny, nz), f32),
            dma((2,)),
            dma((COLS + 1, 2, 2)),
            dma((COLS + 1, 2, 2)),
            dma((2,)),
            dma((2,)),
            dma((n_space * n_tm - 1,)),
            dma((n_space * n_tm - 1,)),
            dma((2, comps)),
        ],
        compiler_params=pltpu.CompilerParams(
            collective_id=0, has_side_effects=True, vmem_limit_bytes=59 << 20
        ),
    )(base, tangent)


def solution(mesh):
    return jax.shard_map(
        functools.partial(body, mesh.shape["tm"], mesh.shape["space"]),
        mesh=mesh,
        in_specs=(P("tm", None, "space", None, None), P("tm", None, None, "space", None, None)),
        out_specs=(
            P("tm", None, "space", None, None),
            P("tm", None, "space", None, None),
            P("tm", None),
        ),
        check_vma=False,
    )
```

```python
import functools

import jax
import jax.numpy as jnp
from jax import lax
from jax.experimental import pallas as pl
from jax.experimental.pallas import tpu as pltpu
from jax.sharding import PartitionSpec as P

MESH = pl.DeviceIdType.MESH
STEPS = 3
COLS = 4
LANES = 128
GRAM = COLS * COLS
ENTRIES = GRAM + COLS * (COLS + 1)
ROWS = 40

time_step = 0.05
viscosity = 0.4
forcing_amp = 1.0
wave_number = 4.0

KEEP = 1.0 - 6.0 * time_step * viscosity
SPREAD = time_step * viscosity
HALF = 0.5 * time_step


def neighbours(ref, lead, plane):
    centre = ref[(*lead, plane)]
    rows, lanes = centre.shape
    east = ref[(*lead, plane + 1)]
    west = ref[(*lead, plane - 1)]
    north = pltpu.roll(centre, rows - 1, 0)
    south = pltpu.roll(centre, 1, 0)
    upper = pltpu.roll(centre, lanes - 1, 1)
    lower = pltpu.roll(centre, 1, 1)
    total = (east + west) + (north + south) + (upper + lower)
    return centre, total, east - west, north - south, upper - lower


def dot_tiles(a, b):
    prod = a * b
    return jnp.sum(prod.reshape(prod.shape[0] // 8, 8, prod.shape[1]), axis=0)


def eliminate(rows, pivoting):
    rows = [list(r) for r in rows]
    n = len(rows)
    for k in range(n):
        if pivoting:
            for r in range(k + 1, n):
                swap = jnp.abs(rows[r][k]) > jnp.abs(rows[k][k])
                for c in range(k, len(rows[k])):
                    high, low = rows[k][c], rows[r][c]
                    rows[k][c] = jnp.where(swap, low, high)
                    rows[r][c] = jnp.where(swap, high, low)
        inverse = 1.0 / rows[k][k]
        for c in range(k + 1, len(rows[k])):
            rows[k][c] = rows[k][c] * inverse
        for r in range(n):
            if r != k:
                factor = rows[r][k]
                for c in range(k + 1, len(rows[k])):
                    rows[r][c] = rows[r][c] - factor * rows[k][c]
    return [r[n:] for r in rows]


def shooting_coefs(entry, n_tm):
    def roll(x, by):
        return pltpu.roll(x, by % LANES, 1)

    gram = [[roll(entry(a * COLS + b), -1) for b in range(COLS)] for a in range(COLS)]
    cross = [[entry(GRAM + k * COLS + j) for k in range(COLS + 1)] for j in range(COLS)]
    maps = eliminate([g + c for g, c in zip(gram, cross)], False)
    maps = [[roll(x, 1) for x in row] for row in maps]
    for level in range(n_tm.bit_length() - 1):
        earlier = [[roll(x, 1 << level) for x in row] for row in maps]
        new = []
        for r in range(COLS):
            row = []
            for c in range(COLS + 1):
                terms = [maps[r][k] * earlier[k][c] for k in range(COLS)]
                value = (terms[0] + terms[1]) + (terms[2] + terms[3])
                row.append(value + maps[r][COLS] if c == COLS else value)
            new.append(row)
        maps = new
    system = [
        [(1.0 if r == c else 0.0) - maps[r][c] for c in range(COLS)] + [maps[r][COLS]]
        for r in range(COLS)
    ]
    return [r[0] for r in eliminate(system, True)]


def kernel(
    n_tm, n_space, base_ref, tangent_ref, push_out, gap_out, next_out, values_ref,
    flow, grads, tang, work, push, base_next, tang_next, acc, table,
    local_sem, send_sem, recv_sem, tm_send, tm_recv,
    table_send, table_recv, near, out_sem,
):
    tm, space = lax.axis_index("tm"), lax.axis_index("space")
    nx = base_ref.shape[2]
    ny, nz = base_ref.shape[3:]
    wide = nx + 2 * STEPS
    up, down = lax.rem(space + 1, n_space), lax.rem(space + n_space - 1, n_space)
    before = lax.rem(tm + n_tm - 1, n_tm)

    barrier = pltpu.get_barrier_semaphore()
    order = sorted(range(n_space), key=lambda d: (d in (0,), min(d, n_space - d)))
    others = [(d, e) for d in order for e in range(n_tm) if (d, e) != (0, 0)]

    def other(offset):
        d, e = offset
        return {"tm": lax.rem(tm + e, n_tm), "space": lax.rem(space + d, n_space)}

    beside = ({"space": up}, {"space": down}, {"tm": lax.rem(tm + 1, n_tm)}, {"tm": before})
    for device in beside:
        pl.semaphore_signal(barrier, inc=1, device_id=device, device_id_type=MESH)
    own = pl.ds(STEPS, nx)
    local = [
        pltpu.make_async_copy(base_ref.at[0], flow.at[0, :, own], local_sem.at[0]),
        pltpu.make_async_copy(tangent_ref.at[0], tang.at[:, :, own], local_sem.at[1]),
    ]
    for copy in local:
        copy.start()
    pl.semaphore_wait(barrier, len(beside))

    def halo(chunk, part, side):
        near = STEPS - 1
        source = (
            (pl.ds(nx - near, near), pl.ds(0, near)),
            (pl.ds(nx - STEPS, 1), pl.ds(near, 1)),
        )[part][side]
        target = (
            (pl.ds(1, near), pl.ds(nx + STEPS, near)),
            (pl.ds(0, 1), pl.ds(wide - 1, 1)),
        )[part][side]
        if isinstance(chunk, int) and chunk == 0:
            src, dst = base_ref.at[0, :, source], flow.at[0, :, target]
        else:
            src, dst = tangent_ref.at[0, chunk - 1, :, source], tang.at[chunk - 1, :, target]
        return pltpu.make_async_remote_copy(
            src_ref=src, dst_ref=dst,
            send_sem=send_sem.at[chunk, part, side], recv_sem=recv_sem.at[chunk, part, side],
            device_id={"space": up if side == 0 else down}, device_id_type=MESH,
        )

    def tm_copy(which):
        src, dst = ((base_ref.at[0], base_next), (tangent_ref.at[0], tang_next))[which]
        return pltpu.make_async_remote_copy(
            src_ref=src, dst_ref=dst, send_sem=tm_send.at[which], recv_sem=tm_recv.at[which],
            device_id={"tm": before}, device_id_type=MESH,
        )

    for chunk in range(COLS + 1):
        for part in (0, 1):
            for side in (0, 1):
                halo(chunk, part, side).start()
    for which in (0, 1):
        tm_copy(which).start()

    def pass_on(i, carry):
        for side, device in enumerate(beside):
            pl.semaphore_signal(near.at[side ^ 1], inc=1, device_id=device, device_id_type=MESH)
        for side in range(len(beside)):
            pl.semaphore_wait(near.at[side], 1)
        return carry

    lax.fori_loop(0, n_space // 2 + n_tm // 2 - 1, pass_on, 0)

    height = lax.broadcasted_iota(jnp.int32, (ny, nz), 0).astype(jnp.float32)
    drive = (time_step * forcing_amp) * jnp.sin(2.0 * jnp.pi * wave_number * height / ny)

    for copy in local:
        copy.wait()
    acc[...] = jnp.zeros_like(acc)
    pairs = [(a, b) for a in range(COLS) for b in range(a, COLS)]

    def gram_step(i, sums):
        comp, plane = i // nx, i % nx + STEPS
        cols = [tang[k, comp, plane] for k in range(COLS)]
        return tuple(s + dot_tiles(cols[a], cols[b]) for s, (a, b) in zip(sums, pairs))

    zero = jnp.zeros((8, nz), jnp.float32)
    sums = lax.fori_loop(0, 3 * nx, gram_step, (zero,) * len(pairs))
    for s, (a, b) in zip(sums, pairs):
        acc[a * COLS + b] = s
        if a != b:
            acc[b * COLS + a] = s

    for part in (0, 1):
        for side in (0, 1):
            halo(0, part, side).wait()
    for t in range(STEPS):

        def flow_step(plane, carry):
            speed = [HALF * flow[t, d, plane] for d in range(3)]
            for c in range(3):
                centre, total, *diffs = neighbours(flow, (t, c), plane)
                value = KEEP * centre + SPREAD * total
                value = value - (speed[0] * diffs[0] + speed[1] * diffs[1] + speed[2] * diffs[2])
                if c == 0:
                    value = value + drive
                flow[t + 1, c, plane] = value
                for d in range(3):
                    grads[t, 3 * c + d, plane] = HALF * diffs[d]
            return carry

        lax.fori_loop(t + 1, wide - t - 1, flow_step, 0)

    for which in (0, 1):
        tm_copy(which).wait()

    def end_step(i, sums):
        comp, plane = i // nx, i % nx
        gap = flow[STEPS, comp, plane + STEPS] - base_next[comp, plane]
        base_next[comp, plane] = gap
        return tuple(s + dot_tiles(tang_next[j, comp, plane], gap) for j, s in enumerate(sums))

    sums = lax.fori_loop(0, 3 * nx, end_step, (zero,) * COLS)
    for j, s in enumerate(sums):
        acc[GRAM + COLS * COLS + j] = s

    gap_copy = pltpu.make_async_copy(base_next, gap_out, out_sem.at[COLS])
    next_copy = pltpu.make_async_copy(tang_next, next_out, out_sem.at[COLS + 1])
    gap_copy.start()
    next_copy.start()

    def push_copy(k):
        return pltpu.make_async_copy(push.at[k], push_out.at[k], out_sem.at[k])

    def column(k, carry):
        def tangent_step(t, plane, sums):
            src, lead = (tang, (k,)) if t == 0 else (work, (t - 1,))
            speed = [HALF * flow[t, d, plane] for d in range(3)]
            own_at = [src[(*lead, d, plane)] for d in range(3)]
            for c in range(3):
                centre, total, *diffs = neighbours(src, (*lead, c), plane)
                value = KEEP * centre + SPREAD * total
                value = value - (
                    speed[0] * diffs[0] + speed[1] * diffs[1] + speed[2] * diffs[2]
                )
                value = value - (
                    own_at[0] * grads[t, 3 * c, plane]
                    + own_at[1] * grads[t, 3 * c + 1, plane]
                    + own_at[2] * grads[t, 3 * c + 2, plane]
                )
                if t < STEPS - 1:
                    work[t, c, plane] = value
                else:
                    push[k, c, plane - STEPS] = value
                    sums = tuple(
                        s + dot_tiles(tang_next[j, c, plane - STEPS], value)
                        for j, s in enumerate(sums)
                    )
            return sums

        sums = (zero,) * COLS
        for part in (0, 1):
            for side in (0, 1):
                halo(k + 1, part, side).wait()
            for t in range(STEPS):
                carried = sums if t == STEPS - 1 else ()
                first, last = t + 1, wide - t - 2
                if part == 0:
                    done = lax.fori_loop(
                        first + 1, last, functools.partial(tangent_step, t), carried
                    )
                else:
                    done = lax.fori_loop(
                        0, 2,
                        lambda i, x, t=t, first=first, last=last: tangent_step(
                            t, first + i * (last - first), x
                        ),
                        carried,
                    )
                if t == STEPS - 1:
                    sums = done
        for j, s in enumerate(sums):
            acc[GRAM + k * COLS + j] = s
        push_copy(k).start()
        return carry

    lax.fori_loop(0, COLS, column, 0)

    by_entry = jnp.sum(jnp.sum(acc[...], axis=1), axis=1, keepdims=True)
    row_id = lax.broadcasted_iota(jnp.int32, (ROWS, LANES), 0)
    lane_id = lax.broadcasted_iota(jnp.int32, (ROWS, LANES), 1)
    packed = jnp.sum(jnp.where(row_id == lane_id, by_entry, 0.0), axis=0, keepdims=True)
    table[space, pl.ds(tm, 1)] = packed

    def table_copy(index):
        row = table.at[space, pl.ds(tm, 1)]
        return pltpu.make_async_remote_copy(
            src_ref=row, dst_ref=row, send_sem=table_send.at[index], recv_sem=table_recv.at[index],
            device_id=other(others[index]), device_id_type=MESH,
        )

    for index in range(len(others)):
        table_copy(index).start()
    for index in range(len(others)):
        table_copy(index).wait()
    summed = functools.reduce(jnp.add, [table[d] for d in range(n_space)])
    square = jnp.concatenate([summed] * (LANES // n_tm), axis=0)
    flipped = square.T
    coefs = shooting_coefs(lambda e: flipped[e : e + 1], n_tm)

    lane = lax.broadcasted_iota(jnp.int32, (1, LANES), 1)
    mine = lane == tm
    following = lane == lax.rem(tm + 1, n_tm)
    both = jnp.concatenate(
        [jnp.where(mine, x, 0.0) for x in coefs] + [jnp.where(following, x, 0.0) for x in coefs],
        axis=0,
    )
    values = jnp.sum(both, axis=1, keepdims=True)
    values_ref[...] = jnp.broadcast_to(values, (2 * COLS, LANES))
    for k in range(COLS):
        push_copy(k).wait()
    gap_copy.wait()
    next_copy.wait()


def finish_kernel(tang, push, gap, tang_next, values, corr, defect, coefs):
    nx, ny, nz = gap.shape[1:]
    places = lax.broadcasted_iota(jnp.int32, (1, COLS), 1)
    out = jnp.zeros((1, COLS), jnp.float32)
    for k in range(COLS):
        out = jnp.where(places == k, values[k : k + 1, :COLS], out)
    coefs[...] = out
    own = [jnp.broadcast_to(values[k : k + 1], (8, LANES)) for k in range(COLS)]
    following = [jnp.broadcast_to(values[COLS + k : COLS + k + 1], (8, LANES)) for k in range(COLS)]

    def scaled(coef, array):
        return (array.reshape(ny // 8, 8, nz) * coef[None]).reshape(ny, nz)

    def finish(plane, carry):
        terms = [scaled(own[k], tang[0, k, 0, plane]) for k in range(COLS)]
        corr[0, 0, plane] = (terms[0] + terms[1]) + (terms[2] + terms[3])
        value = gap[0, plane]
        for k in range(COLS):
            value = value + (
                scaled(own[k], push[k, 0, plane]) - scaled(following[k], tang_next[k, 0, plane])
            )
        defect[0, 0, plane] = value
        return carry

    lax.fori_loop(0, nx, finish, 0)


def body(n_tm, n_space, base, tangent):
    _, comps, nx, ny, nz = base.shape
    wide = nx + 2 * STEPS
    f32 = jnp.float32
    vmem = pltpu.VMEM
    dma = pltpu.SemaphoreType.DMA
    anywhere = pl.BlockSpec(memory_space=pl.ANY)
    push, gap, tang_next, values = pl.pallas_call(
        functools.partial(kernel, n_tm, n_space),
        out_shape=(
            jax.ShapeDtypeStruct((COLS, comps, nx, ny, nz), f32),
            jax.ShapeDtypeStruct((comps, nx, ny, nz), f32),
            jax.ShapeDtypeStruct((COLS, comps, nx, ny, nz), f32),
            jax.ShapeDtypeStruct((2 * COLS, LANES), f32),
        ),
        in_specs=[anywhere, anywhere],
        out_specs=(anywhere, anywhere, anywhere, pl.BlockSpec(memory_space=pltpu.VMEM)),
        scratch_shapes=[
            vmem((STEPS + 1, comps, wide, ny, nz), f32),
            vmem((STEPS, 3 * comps, wide, ny, nz), f32),
            vmem((COLS, comps, wide, ny, nz), f32),
            vmem((STEPS - 1, comps, wide, ny, nz), f32),
            vmem((COLS, comps, nx, ny, nz), f32),
            vmem((comps, nx, ny, nz), f32),
            vmem((COLS, comps, nx, ny, nz), f32),
            vmem((ROWS, 8, nz), f32),
            vmem((n_space, n_tm, LANES), f32),
            dma((2,)),
            dma((COLS + 1, 2, 2)),
            dma((COLS + 1, 2, 2)),
            dma((2,)),
            dma((2,)),
            dma((n_space * n_tm - 1,)),
            dma((n_space * n_tm - 1,)),
            pltpu.SemaphoreType.REGULAR((4,)),
            dma((COLS + 2,)),
        ],
        compiler_params=pltpu.CompilerParams(
            collective_id=0, has_side_effects=True, vmem_limit_bytes=44 << 20
        ),
    )(pltpu.with_memory_space_constraint(base, pltpu.HBM), pltpu.with_memory_space_constraint(tangent, pltpu.HBM))
    block = (nx, ny, nz)
    columns = pl.BlockSpec((COLS, 1, *block), lambda c: (0, c, 0, 0, 0))
    field = pl.BlockSpec((1, 1, *block), lambda c: (0, c, 0, 0, 0))
    return pl.pallas_call(
        finish_kernel,
        grid=(comps,),
        out_shape=(
            jax.ShapeDtypeStruct(base.shape, f32),
            jax.ShapeDtypeStruct(base.shape, f32),
            jax.ShapeDtypeStruct((1, COLS), f32),
        ),
        in_specs=[
            pl.BlockSpec((1, COLS, 1, *block), lambda c: (0, 0, c, 0, 0, 0)),
            columns,
            pl.BlockSpec((1, *block), lambda c: (c, 0, 0, 0)),
            columns,
            pl.BlockSpec((2 * COLS, LANES), lambda c: (0, 0)),
        ],
        out_specs=(field, field, pl.BlockSpec((1, COLS), lambda c: (0, 0))),
        compiler_params=pltpu.CompilerParams(vmem_limit_bytes=24 << 20),
    )(tangent, push, gap, tang_next, values)


def solution(mesh):
    return jax.shard_map(
        functools.partial(body, mesh.shape["tm"], mesh.shape["space"]),
        mesh=mesh,
        in_specs=(P("tm", None, "space", None, None), P("tm", None, None, "space", None, None)),
        out_specs=(
            P("tm", None, "space", None, None),
            P("tm", None, "space", None, None),
            P("tm", None),
        ),
        check_vma=False,
    )
```
